256 devices in a mesh: row: 16 (over x, z_lo, core), col: 16 (over y, z_hi).
Axes of the slice: x: 4, y: 4, z: 8 (z_hi: 4, z_lo: 2; z = z_hi * 2 + z_lo), core: 2. Of those that a mesh axis runs over, the one named last changes fastest.
Arguments:
- velocity: float32 [3, 128, 256, 1536], P(None, 'col', None, 'row'), may hold values from -6 to 6
- dx_matrix: float32 [256, 256], replicated, may hold values from -0.375 to 0.375
- dy_matrix: float32 [1536, 1536], replicated, may hold values from -0.15625 to 0.15625
- dz_matrix: float32 [128, 128], replicated, may hold values from -0.5 to 0.5
- metric: float32 [1536], replicated, may hold values from 0.5 to 2
Outputs:
- convective: float32 [3, 128, 256, 1536], P(None, None, 'row', 'col')
The draws below stay inside these ranges and needn't reach their ends.
All inputs are finite; a program needn't handle non-finite values.
Results may differ from the reference program's by a relative error of at most 0.000092.
Values sent between devices are 32-bit elements; how exact they have to be, the bound alone decides.
No kernel may reach another device: no remote copies, remote signals or barrier semaphores. Data moves between devices by JAX's collectives and lax.ppermute only.
A program may use at most 128 MiB of HBM per device.

```python
import math
import jax
import jax.numpy as jnp
from jax import lax

NY = 1536
NX = 256
NZ = 128


def block_scale(rng, shape, split, smallest, high):
    factor_of = 1.0
    for position, blocks in split:
        heights = jax.random.uniform(jax.random.fold_in(jax.random.fold_in(rng, 6), position), (blocks,), jnp.float32, smallest / len(split), high / len(split))
        factor_of = factor_of * jnp.repeat(jnp.exp(heights), shape[position] // blocks).reshape((-1,) + (1,) * (len(shape) - 1 - position))
    return factor_of


def bell_draw(rng, extent, deviation, bound, cuts=(), kind=jnp.bfloat16):
    entries = jax.random.normal(rng, extent, jnp.float32) * deviation
    if len(cuts) > 0:
        entries = block_scale(rng, extent, cuts, -0.22, 0.18) * entries
    return jnp.clip(entries, min=-bound, max=bound).astype(kind)


def setup_inputs(seed: int = 0) -> dict:
    seeds = jax.random.split(jax.random.key(seed), 6)
    velocity = bell_draw(seeds[0], (3, NZ, NX, NY), 1.0, 6.0, ((1, 16), (3, 16)), jnp.float32)
    dx_matrix = bell_draw(seeds[1], (NX, NX), NX ** -0.5, 0.375, (), jnp.float32)
    dy_matrix = bell_draw(seeds[2], (NY, NY), NY ** -0.5, 0.15625, (), jnp.float32)
    dz_matrix = bell_draw(seeds[3], (NZ, NZ), NZ ** -0.5, 0.5, (), jnp.float32)
    metric = jnp.clip(jnp.exp(jax.random.uniform(seeds[4], (NY,), jnp.float32, math.log(0.5), math.log(2.0))), 0.5, 2.0)
    return dict(velocity=velocity, dx_matrix=dx_matrix, dy_matrix=dy_matrix, dz_matrix=dz_matrix, metric=metric)


def reference(velocity, dx_matrix, dy_matrix, dz_matrix, metric):
    high = lax.Precision.HIGHEST
    deriv_x = jnp.einsum('czxy,Xx->czXy', velocity, dx_matrix, precision=high)
    partial_value = velocity[0][None] * deriv_x
    deriv_y = jnp.einsum('czxy,Yy->czxY', velocity, dy_matrix, precision=high)
    deriv_y = deriv_y * metric
    partial_value = partial_value + velocity[1][None] * deriv_y
    deriv_z = jnp.einsum('czxy,Zz->cZxy', velocity, dz_matrix, precision=high)
    return partial_value + velocity[2][None] * deriv_z
```

```python
import functools

import jax
import jax.numpy as jnp
from jax import lax
from jax.experimental import pallas as pl
from jax.experimental.pallas import tpu as pltpu
from jax.sharding import PartitionSpec as P

NB, NC, YB, LN = 16, 3, 96, 128
ZB, NX, NY = 8, 256, 1536
VMEM_LIMIT = 56 * 1024 * 1024


def swap_bits(arrs, dist, shift, lane):
    low = (lane & shift) == 0
    out = list(arrs)
    for i in range(len(arrs)):
        if i & dist == 0:
            a, b = arrs[i], arrs[i | dist]
            out[i] = jnp.where(low, a, pltpu.roll(b, shift, 1))
            out[i | dist] = jnp.where(low, pltpu.roll(a, LN - shift, 1), b)
    return out


def split(v):
    high = v.astype(jnp.bfloat16)
    return high, (v - high.astype(jnp.float32)).astype(jnp.bfloat16)


def dot3(a, b, dims):
    dot = lambda x, y: lax.dot_general(x, y, (dims, ((), ())), preferred_element_type=jnp.float32)
    return dot(a[0], b[0]) + (dot(a[0], b[1]) + dot(a[1], b[0]))


def lanes8():
    return lax.broadcasted_iota(jnp.int32, (8, LN), 1)


def x_to_blocks(load, store):
    lane = lanes8()

    def body(t, _):
        rows = pl.ds(pl.multiple_of(t * 8, 8), 8)
        for half in range(2):
            arrs = [load(z, rows, half) for z in range(ZB)]
            for k in (2, 1, 0):
                arrs = swap_bits(arrs, 1 << k, 1 << k, lane)
                arrs = swap_bits(arrs, 1 << k, 16 << k, lane)
            for i in range(8):
                store(half * 8 + i, rows, arrs[i])
        return 0

    lax.fori_loop(0, YB // 8, body, 0)


def pack_kernel(v_ref, out_ref):
    def load(z, rows, half):
        return v_ref[0, z, rows, half * LN : (half + 1) * LN]

    def store(block, rows, value):
        out_ref[block, 0, rows, :] = value

    x_to_blocks(load, store)


def x_kernel(v_ref, u_ref, dx_ref, out_ref, part_ref):
    d = split(dx_ref[...])
    deriv = dot3(split(v_ref[0].reshape(ZB * YB, NX)), d, ((1,), (1,)))
    part_ref[...] = u_ref[0] * deriv.reshape(ZB, YB, NX)

    def load(z, rows, half):
        return part_ref[z, rows, half * LN : (half + 1) * LN]

    def store(block, rows, value):
        out_ref[block, 0, rows, :] = value

    x_to_blocks(load, store)


def y_kernel(v_ref, dy_ref, metric_ref, out_ref, vh_ref, vl_ref):
    step = pl.program_id(0)

    @pl.when(step == 0)
    def _():
        for c in range(NC):
            high, low = split(v_ref[:, c].reshape(NY, LN))
            vh_ref[:, c * LN : (c + 1) * LN] = high
            vl_ref[:, c * LN : (c + 1) * LN] = low

    nb = out_ref.shape[0]
    deriv = dot3(split(dy_ref[...]), (vh_ref[...], vl_ref[...]), ((1,), (0,)))
    v1 = v_ref[pl.ds(step * nb, nb), 1].reshape(nb * YB, LN) * metric_ref[...]
    for c in range(NC):
        out_ref[:, c] = (v1 * deriv[:, c * LN : (c + 1) * LN]).reshape(nb, YB, LN)


def z_to_lanes(load, store):
    lane = lanes8()

    def body(t, _):
        rows = pl.ds(pl.multiple_of(t * 8, 8), 8)
        arrs = [load(s, rows) for s in range(NB)]
        for k in range(4):
            arrs = swap_bits(arrs, 1 << k, 8 << k, lane)
        for i in range(NB):
            store((i >> 1) | ((i & 1) << 3), rows, arrs[i])
        return 0

    lax.fori_loop(0, YB // 8, body, 0)


def z_kernel(v_ref, dz_ref, out_ref, w_ref, t_ref):
    d = split(dz_ref[...])

    def gather(c, dst):
        def store(x, rows, value):
            dst[x, rows, :] = value

        z_to_lanes(lambda s, rows: v_ref[s, c, rows, :], store)

    gather(2, w_ref)
    for c in range(NC):
        src = w_ref
        if c < 2:
            gather(c, t_ref)
            src = t_ref
        deriv = dot3(split(src[...].reshape(NB * YB, LN)), d, ((1,), (1,)))
        out_ref[c] = w_ref[...] * deriv.reshape(NB, YB, LN)


def add_kernel(a_ref, w_ref, out_ref):
    def store(x, rows, value):
        out_ref[0, x, rows, :] = value + w_ref[0, x, rows, :]

    z_to_lanes(lambda s, rows: a_ref[s, 0, rows, :], store)


def call(kernel, flops=0, nbytes=0, **kw):
    return pl.pallas_call(
        kernel,
        compiler_params=pltpu.CompilerParams(vmem_limit_bytes=VMEM_LIMIT),
        cost_estimate=pl.CostEstimate(flops=flops, bytes_accessed=nbytes, transcendentals=0),
        **kw,
    )


def per_device(velocity, dx_matrix, dy_matrix, dz_matrix, metric):
    f32 = jnp.float32
    blocks = jax.ShapeDtypeStruct((NB, NC, YB, LN), f32)
    size = NB * NC * YB * LN * 4
    v = jnp.transpose(velocity, (0, 1, 3, 2))
    in_spec = pl.BlockSpec((1, ZB, YB, NX), lambda c: (c, 0, 0, 0))
    out_spec = pl.BlockSpec((NB, 1, YB, LN), lambda c: (0, c, 0, 0))
    packed = call(pack_kernel, 0, 2 * size, grid=(NC,), in_specs=[in_spec], out_specs=out_spec, out_shape=blocks)(v)
    v_y = lax.all_to_all(packed, "row", split_axis=0, concat_axis=0, tiled=True)
    part = call(
        x_kernel,
        6 * NC * ZB * YB * NX * NX,
        2 * size,
        grid=(NC,),
        in_specs=[
            in_spec,
            pl.BlockSpec((1, ZB, YB, NX), lambda c: (0, 0, 0, 0)),
            pl.BlockSpec((NX, NX), lambda c: (0, 0)),
        ],
        out_specs=out_spec,
        out_shape=blocks,
        scratch_shapes=[pltpu.VMEM((ZB, YB, NX), f32)],
    )(v, v, dx_matrix)
    part_y = lax.all_to_all(part, "row", split_axis=0, concat_axis=0, tiled=True)
    v_z = lax.all_to_all(v_y, "col", split_axis=0, concat_axis=0, tiled=True)
    yb = 4
    term_y = call(
        y_kernel,
        6 * NY * NY * NC * LN,
        2 * size + NY * NY * 4,
        grid=(NB // yb,),
        in_specs=[
            pl.BlockSpec((NB, NC, YB, LN), lambda i: (0, 0, 0, 0)),
            pl.BlockSpec((yb * YB, NY), lambda i: (i, 0)),
            pl.BlockSpec((yb * YB, LN), lambda i: (i, 0)),
        ],
        out_specs=pl.BlockSpec((yb, NC, YB, LN), lambda i: (i, 0, 0, 0)),
        out_shape=blocks,
        scratch_shapes=[pltpu.VMEM((NY, NC * LN), jnp.bfloat16)] * 2,
    )(v_y, dy_matrix, jnp.broadcast_to(metric[:, None], (NY, LN)))
    accum_z = lax.all_to_all(part_y + term_y, "col", split_axis=0, concat_axis=0, tiled=True)
    pencils = jax.ShapeDtypeStruct((NC, NB, YB, LN), f32)
    term_z = call(
        z_kernel,
        6 * NC * NB * YB * LN * LN,
        2 * size,
        grid=(1,),
        in_specs=[
            pl.BlockSpec((NB, NC, YB, LN), lambda i: (0, 0, 0, 0)),
            pl.BlockSpec((LN, LN), lambda i: (0, 0)),
        ],
        out_specs=pl.BlockSpec((NC, NB, YB, LN), lambda i: (0, 0, 0, 0)),
        out_shape=pencils,
        scratch_shapes=[pltpu.VMEM((NB, YB, LN), f32)] * 2,
    )(v_z, dz_matrix)
    pencil_spec = pl.BlockSpec((1, NB, YB, LN), lambda c: (c, 0, 0, 0))
    out = call(
        add_kernel,
        0,
        3 * size,
        grid=(NC,),
        in_specs=[out_spec, pencil_spec],
        out_specs=pencil_spec,
        out_shape=pencils,
    )(accum_z, term_z)
    return jnp.transpose(out, (0, 3, 1, 2))


def solution(mesh):
    return jax.shard_map(
        per_device,
        mesh=mesh,
        in_specs=(P(None, "col", None, "row"), P(), P(), P(), P()),
        out_specs=P(None, None, "row", "col"),
        check_vma=False,
    )
```

```python
import jax
import jax.numpy as jnp
from jax import lax
from jax.experimental import pallas as pl
from jax.experimental.pallas import tpu as pltpu
from jax.sharding import PartitionSpec as P

NB, NC, YB, LN = 16, 3, 96, 128
ZB, NX, NY = 8, 256, 1536
SIZE = NB * NC * YB * LN * 4
BLOCKS = jax.ShapeDtypeStruct((NB, NC, YB, LN), jnp.float32)
PENCILS = jax.ShapeDtypeStruct((NC, NB, YB, LN), jnp.float32)
VMEM = pl.BlockSpec(memory_space=pltpu.VMEM)
SMEM = pl.BlockSpec(memory_space=pltpu.SMEM)


def call(kernel, flops=0, nbytes=0, **kw):
    return pl.pallas_call(
        kernel,
        compiler_params=pltpu.CompilerParams(vmem_limit_bytes=24 * 1024 * 1024),
        cost_estimate=pl.CostEstimate(flops=flops, bytes_accessed=nbytes, transcendentals=0),
        **kw,
    )


def lanes8():
    return lax.broadcasted_iota(jnp.int32, (8, LN), 1)


def swap_bits(arrs, dist, shift, lane):
    low = (lane & shift) == 0
    out = list(arrs)
    for i in range(len(arrs)):
        if i & dist == 0:
            a, b = arrs[i], arrs[i | dist]
            out[i] = jnp.where(low, a, pltpu.roll(b, shift, 1))
            out[i | dist] = jnp.where(low, pltpu.roll(a, LN - shift, 1), b)
    return out


def zx_to_xz(a, lane):
    return jnp.take_along_axis(a, ((lane & 7) << 4) | (lane & 8) | (lane >> 4), axis=1)


def over_rows(nc, body, unroll=3):
    tiles = YB // 8

    def step(i, _):
        body(i // tiles, pl.ds(pl.multiple_of(i % tiles * 8, 8), 8))
        return 0

    lax.fori_loop(0, nc * tiles, step, 0, unroll=unroll)


def split(v):
    high = v.astype(jnp.bfloat16)
    return high, (v - high.astype(jnp.float32)).astype(jnp.bfloat16)


def dot3(a, b, dims):
    dot = lambda x, y: lax.dot_general(x, y, (dims, ((), ())), preferred_element_type=jnp.float32)
    return dot(a[0], b[0]) + (dot(a[0], b[1]) + dot(a[1], b[0]))


def x_to_blocks(load, lane, half):
    arrs = [load(z, half) for z in range(ZB)]
    for k in (2, 1, 0):
        arrs = swap_bits(arrs, 1 << k, 16 << k, lane)
    return arrs


def pack_kernel(v_ref, out_ref):
    lane = lanes8()

    def body(c, rows):
        for half in range(2):
            arrs = x_to_blocks(lambda z, h: v_ref[c, z, rows, h * LN : (h + 1) * LN], lane, half)
            for i in range(8):
                out_ref[half * 8 + i, c, rows, :] = arrs[i]

    over_rows(NC, body)


def pack(v):
    return call(pack_kernel, 0, 2 * SIZE, in_specs=[VMEM], out_specs=VMEM, out_shape=BLOCKS)(v)


def x_kernel(v_ref, dx_ref, out_ref, part_ref):
    d = split(dx_ref[...])
    for c in range(NC):
        deriv = dot3(split(v_ref[c].reshape(ZB * YB, NX)), d, ((1,), (1,)))
        part_ref[c] = v_ref[0] * deriv.reshape(ZB, YB, NX)
    lane = lanes8()

    def body(c, rows):
        for half in range(2):
            arrs = x_to_blocks(lambda z, h: part_ref[c, z, rows, h * LN : (h + 1) * LN], lane, half)
            for i in range(8):
                out_ref[half * 8 + i, c, rows, :] = zx_to_xz(arrs[i], lane)

    over_rows(NC, body)


def x_term(v, dx_matrix):
    return call(
        x_kernel,
        6 * NC * ZB * YB * NX * NX,
        2 * SIZE,
        in_specs=[VMEM, VMEM],
        out_specs=VMEM,
        out_shape=BLOCKS,
        scratch_shapes=[pltpu.VMEM((NC, ZB, YB, NX), jnp.float32)],
    )(v, dx_matrix)


def y_kernel(v_ref, dy_ref, metric_ref, out_ref, vh_ref, vl_ref, t_ref):
    step = pl.program_id(0)

    @pl.when(step == 0)
    def _():
        for c in range(NC):
            high, low = split(v_ref[:, c].reshape(NY, LN))
            vh_ref[:, c * LN : (c + 1) * LN] = high
            vl_ref[:, c * LN : (c + 1) * LN] = low

    nb = out_ref.shape[0]
    deriv = dot3(split(dy_ref[...]), (vh_ref[...], vl_ref[...]), ((1,), (0,)))
    v1 = v_ref[pl.ds(step * nb, nb), 1].reshape(nb * YB, LN) * metric_ref[...]
    for c in range(NC):
        t_ref[:, c] = (v1 * deriv[:, c * LN : (c + 1) * LN]).reshape(nb, YB, LN)
    lane = lanes8()

    def body(c, rows):
        for b in range(nb):
            out_ref[b, c, rows, :] = zx_to_xz(t_ref[b, c, rows, :], lane)

    over_rows(NC, body)


def y_term(v_y, dy_matrix, metric):
    nb = 4
    return call(
        y_kernel,
        6 * NY * NY * NC * LN,
        2 * SIZE + NY * NY * 4,
        grid=(NB // nb,),
        in_specs=[
            pl.BlockSpec((NB, NC, YB, LN), lambda i: (0, 0, 0, 0)),
            pl.BlockSpec((nb * YB, NY), lambda i: (i, 0)),
            pl.BlockSpec((nb * YB, LN), lambda i: (i, 0)),
        ],
        out_specs=pl.BlockSpec((nb, NC, YB, LN), lambda i: (i, 0, 0, 0)),
        out_shape=BLOCKS,
        scratch_shapes=[pltpu.VMEM((NY, NC * LN), jnp.bfloat16)] * 2
        + [pltpu.VMEM((nb, NC, YB, LN), jnp.float32)],
    )(v_y, dy_matrix, jnp.broadcast_to(metric[:, None], (NY, LN)))


def z_to_lanes(arrs, lane):
    for k in range(4):
        arrs = swap_bits(arrs, 1 << k, 8 << k, lane)
    return [arrs[(x & 7) * 2 + (x >> 3)] for x in range(NB)]


def z_kernel(at_ref, v_ref, dz_ref, out_ref, t_ref):
    d = split(dz_ref[...])
    lane = lanes8()
    at = [at_ref[s] for s in range(NB)]

    def body(c, rows):
        arrs = z_to_lanes([zx_to_xz(v_ref[at[s], c, rows, :], lane) for s in range(NB)], lane)
        for x in range(NB):
            t_ref[c, x, rows, :] = arrs[x]

    over_rows(NC, body)
    for c in range(NC):
        deriv = dot3(split(t_ref[c].reshape(NB * YB, LN)), d, ((1,), (1,)))
        out_ref[c] = t_ref[2] * deriv.reshape(NB, YB, LN)


def z_term(at, v_z, dz_matrix):
    return call(
        z_kernel,
        6 * NC * NB * YB * LN * LN,
        2 * SIZE,
        in_specs=[SMEM, VMEM, VMEM],
        out_specs=VMEM,
        out_shape=PENCILS,
        scratch_shapes=[pltpu.VMEM((NC, NB, YB, LN), jnp.float32)],
    )(at, v_z, dz_matrix)


def finish_kernel(a_ref, w_ref, out_ref):
    lane = lanes8()

    def body(c, rows):
        arrs = z_to_lanes([a_ref[s, c, rows, :] for s in range(NB)], lane)
        for x in range(NB):
            out_ref[c, x, rows, :] = arrs[x] + w_ref[c, x, rows, :]

    over_rows(NC, body)


def finish(accum_z, term_z):
    return call(finish_kernel, 0, 3 * SIZE, in_specs=[VMEM, VMEM], out_specs=VMEM, out_shape=PENCILS)(accum_z, term_z)


def exchange(a, axis):
    return lax.all_to_all(a, axis, split_axis=0, concat_axis=0, tiled=True)


def col_exchange(a, y, h, term):
    a = a.reshape(4, 4, NC, YB, LN)
    along_z = lambda x, s: lax.ppermute(x, "col", [(i * 4 + j, i * 4 + (j + s) % 4) for i in range(4) for j in range(4)])
    along_y = lambda x, s: lax.ppermute(x, "col", [(i * 4 + j, (i + s) % 4 * 4 + j) for i in range(4) for j in range(4)])
    take = lambda x, i, axis: lax.dynamic_index_in_dim(x, i & 3, axis, keepdims=False)
    odd = [along_z(take(a, h + s, 1), s) for s in (1, 3)]
    even = jnp.stack([take(a, h, 1), take(a, h + 2, 1)], axis=1)
    even = [take(even, y, 0)] + [along_y(take(even, y + t, 0), t) for t in (1, 2, 3)]
    two = along_z(jnp.stack([e[1] for e in even]), 2)
    odd, term = lax.optimization_barrier((odd, term))
    odd = jnp.stack(odd, axis=1)
    odd = [take(odd, y, 0)] + [along_y(take(odd, y + t, 0), t) for t in (1, 2, 3)]
    place = lambda t, s: jnp.where(s & 1, 2 * t + (s >> 1), 8 + 2 * s + t)
    at = [place((y - i) & 3, (h - j) & 3) for i in range(4) for j in range(4)]
    return term, odd, [e[0] for e in even], two, jnp.stack(at).astype(jnp.int32)


def per_device(velocity, dx_matrix, dy_matrix, dz_matrix, metric):
    me = lax.axis_index("col")
    v = jnp.transpose(velocity, (0, 1, 3, 2))
    v_y = exchange(pack(v), "row")
    part, v_y = lax.optimization_barrier((x_term(v, dx_matrix), v_y))
    term = y_term(v_y, dy_matrix, metric)
    term, odd, zero, two, at = col_exchange(v_y, me >> 2, me & 3, term)
    accum = exchange(part, "row") + term
    accum, odd, zero, two = lax.optimization_barrier((accum, odd, zero, two))
    accum_z = exchange(accum, "col")
    v_z = jnp.concatenate(odd + [jnp.stack(zero), two])
    return jnp.transpose(finish(accum_z, z_term(at, v_z, dz_matrix)), (0, 3, 1, 2))


def solution(mesh):
    return jax.shard_map(
        per_device,
        mesh=mesh,
        in_specs=(P(None, "col", None, "row"), P(), P(), P(), P()),
        out_specs=P(None, None, "row", "col"),
        check_vma=False,
    )
```

```python
import jax
import jax.numpy as jnp
from jax import lax
from jax.experimental import pallas as pl
from jax.experimental.pallas import tpu as pltpu
from jax.sharding import PartitionSpec as P

NB, NC, YB, LN = 16, 3, 96, 128
ZB, NX, NY = 8, 256, 1536
SIZE = NB * NC * YB * LN * 4
BLOCKS = jax.ShapeDtypeStruct((NB, NC, YB, LN), jnp.float32)
PENCILS = jax.ShapeDtypeStruct((NC, NB, YB, LN), jnp.float32)
VMEM = pl.BlockSpec(memory_space=pltpu.VMEM)
SMEM = pl.BlockSpec(memory_space=pltpu.SMEM)
HBM = pl.BlockSpec(memory_space=pltpu.HBM)


def call(kernel, flops=0, nbytes=0, limit=24, **kw):
    return pl.pallas_call(
        kernel,
        compiler_params=pltpu.CompilerParams(vmem_limit_bytes=limit * 1024 * 1024),
        cost_estimate=pl.CostEstimate(flops=flops, bytes_accessed=nbytes, transcendentals=0),
        **kw,
    )


def lanes8():
    return lax.broadcasted_iota(jnp.int32, (8, LN), 1)


def swap_bits(arrs, dist, shift, lane):
    low = (lane & shift) == 0
    out = list(arrs)
    for i in range(len(arrs)):
        if i & dist == 0:
            a, b = arrs[i], arrs[i | dist]
            out[i] = jnp.where(low, a, pltpu.roll(b, shift, 1))
            out[i | dist] = jnp.where(low, pltpu.roll(a, LN - shift, 1), b)
    return out


def zx_to_xz(lane, block):
    lane = (lane - 8 * block) & (LN - 1)
    return ((lane & 7) << 4) | (lane & 8) | (lane >> 4)


def over_rows(components, body):
    tiles = YB // 8

    def step(i, _):
        body(components[0] + i // tiles, pl.ds(pl.multiple_of(i % tiles * 8, 8), 8))
        return 0

    lax.fori_loop(0, len(components) * tiles, step, 0, unroll=3)


ALL = range(NC)


def split(v):
    high = v.astype(jnp.bfloat16)
    return high, (v - high.astype(jnp.float32)).astype(jnp.bfloat16)


def dot3(a, b, dims):
    dot = lambda x, y: lax.dot_general(x, y, (dims, ((), ())), preferred_element_type=jnp.float32)
    return dot(a[0], b[0]) + (dot(a[0], b[1]) + dot(a[1], b[0]))


def x_to_blocks(load, lane, half):
    arrs = [load(z, half) for z in range(ZB)]
    for k in (2, 1, 0):
        arrs = swap_bits(arrs, 1 << k, 16 << k, lane)
    return arrs


def pack_kernel(v_hbm, out_hbm, v_ref, out_ref, sems):
    lane = lanes8()
    loads = [pltpu.make_async_copy(v_hbm.at[c], v_ref.at[c], sems.at[c]) for c in ALL]
    stores = [pltpu.make_async_copy(out_ref.at[c], out_hbm.at[:, c], sems.at[NC + c]) for c in ALL]
    for load in loads:
        load.start()

    def body(c, rows):
        for half in range(2):
            arrs = x_to_blocks(lambda z, h: v_ref[c, z, rows, h * LN : (h + 1) * LN], lane, half)
            for i in range(8):
                out_ref[c, half * 8 + i, rows, :] = arrs[i]

    for c in ALL:
        loads[c].wait()
        over_rows([c], body)
        stores[c].start()
    for store in stores:
        store.wait()


def pack(v):
    return call(
        pack_kernel,
        0,
        2 * SIZE,
        limit=56,
        in_specs=[HBM],
        out_specs=HBM,
        out_shape=BLOCKS,
        scratch_shapes=[
            pltpu.VMEM((NC, ZB, YB, NX), jnp.float32),
            pltpu.VMEM((NC, NB, YB, LN), jnp.float32),
            pltpu.SemaphoreType.DMA((2 * NC,)),
        ],
    )(v)


def x_kernel(block_ref, v_ref, dx_ref, out_ref, part_ref):
    d = split(dx_ref[...])
    for c in range(NC):
        deriv = dot3(split(v_ref[c].reshape(ZB * YB, NX)), d, ((1,), (1,)))
        part_ref[c] = v_ref[0] * deriv.reshape(ZB, YB, NX)
    lane = lanes8()
    order = zx_to_xz(lane, block_ref[0])

    def body(c, rows):
        for half in range(2):
            arrs = x_to_blocks(lambda z, h: part_ref[c, z, rows, h * LN : (h + 1) * LN], lane, half)
            for i in range(8):
                out_ref[half * 8 + i, c, rows, :] = jnp.take_along_axis(arrs[i], order, axis=1)

    over_rows(ALL, body)


def x_term(block, v, dx_matrix):
    return call(
        x_kernel,
        6 * NC * ZB * YB * NX * NX,
        2 * SIZE,
        in_specs=[SMEM, VMEM, VMEM],
        out_specs=VMEM,
        out_shape=BLOCKS,
        scratch_shapes=[pltpu.VMEM((NC, ZB, YB, NX), jnp.float32)],
    )(block, v, dx_matrix)


def y_kernel(block_ref, v_ref, dy_ref, metric_ref, out_ref, vh_ref, vl_ref, t_ref):
    step = pl.program_id(0)

    @pl.when(step == 0)
    def _():
        for c in range(NC):
            high, low = split(v_ref[:, c].reshape(NY, LN))
            vh_ref[:, c * LN : (c + 1) * LN] = high
            vl_ref[:, c * LN : (c + 1) * LN] = low

    nb = out_ref.shape[0]
    deriv = dot3(split(dy_ref[...]), (vh_ref[...], vl_ref[...]), ((1,), (0,)))
    v1 = v_ref[pl.ds(step * nb, nb), 1].reshape(nb * YB, LN) * metric_ref[...]
    for c in range(NC):
        t_ref[:, c] = (v1 * deriv[:, c * LN : (c + 1) * LN]).reshape(nb, YB, LN)
    order = zx_to_xz(lanes8(), block_ref[0])

    def body(c, rows):
        for b in range(nb):
            out_ref[b, c, rows, :] = jnp.take_along_axis(t_ref[b, c, rows, :], order, axis=1)

    over_rows(ALL, body)


def y_term(block, v_y, dy_matrix, metric):
    nb = 4
    return call(
        y_kernel,
        6 * NY * NY * NC * LN,
        2 * SIZE + NY * NY * 4,
        grid=(NB // nb,),
        in_specs=[
            SMEM,
            pl.BlockSpec((NB, NC, YB, LN), lambda i: (0, 0, 0, 0)),
            pl.BlockSpec((nb * YB, NY), lambda i: (i, 0)),
            pl.BlockSpec((nb * YB, LN), lambda i: (i, 0)),
        ],
        out_specs=pl.BlockSpec((nb, NC, YB, LN), lambda i: (i, 0, 0, 0)),
        out_shape=BLOCKS,
        scratch_shapes=[pltpu.VMEM((NY, NC * LN), jnp.bfloat16)] * 2
        + [pltpu.VMEM((nb, NC, YB, LN), jnp.float32)],
    )(block, v_y, dy_matrix, jnp.broadcast_to(metric[:, None], (NY, LN)))


def z_to_lanes(arrs, lane):
    for k in range(4):
        high = (lane & 8 << k) != 0
        arrs = [jnp.where(high, arrs[(i + (1 << k)) % NB], arrs[i]) for i in range(NB)]
    turned = [pltpu.roll(arrs[-g % NB], (LN - 8 * g) % LN, 1) if g else arrs[0] for g in range(NB)]
    return [turned[(x & 7) * 2 + (x >> 3)] for x in range(NB)]


def z_kernel(at_ref, v_ref, dz_ref, out_ref, t_ref):
    d = split(dz_ref[...])
    lane = lanes8()
    at = [at_ref[s] for s in range(NB)]

    def body(c, rows):
        arrs = [jnp.take_along_axis(v_ref[at[s], c, rows, :], zx_to_xz(lane, s), axis=1) for s in range(NB)]
        arrs = z_to_lanes(arrs, lane)
        for x in range(NB):
            t_ref[c, x, rows, :] = arrs[x]

    over_rows(ALL, body)
    for c in range(NC):
        deriv = dot3(split(t_ref[c].reshape(NB * YB, LN)), d, ((1,), (1,)))
        out_ref[c] = t_ref[2] * deriv.reshape(NB, YB, LN)


def z_term(at, v_z, dz_matrix):
    return call(
        z_kernel,
        6 * NC * NB * YB * LN * LN,
        2 * SIZE,
        in_specs=[SMEM, VMEM, VMEM],
        out_specs=VMEM,
        out_shape=PENCILS,
        scratch_shapes=[pltpu.VMEM((NC, NB, YB, LN), jnp.float32)],
    )(at, v_z, dz_matrix)


def finish_kernel(a_ref, w_hbm, out_hbm, w_ref, sems):
    lane = lanes8()
    loads = [pltpu.make_async_copy(w_hbm.at[c], w_ref.at[c], sems.at[c]) for c in ALL]
    stores = [pltpu.make_async_copy(w_ref.at[c], out_hbm.at[c], sems.at[NC + c]) for c in ALL]
    for load in loads:
        load.start()

    def body(c, rows):
        arrs = z_to_lanes([a_ref[s, c, rows, :] for s in range(NB)], lane)
        for x in range(NB):
            w_ref[c, x, rows, :] += arrs[x]

    for c in ALL:
        loads[c].wait()
        over_rows([c], body)
        stores[c].start()
    for store in stores:
        store.wait()


def finish(accum_z, term_z):
    return call(
        finish_kernel,
        0,
        3 * SIZE,
        in_specs=[VMEM, HBM],
        out_specs=HBM,
        out_shape=PENCILS,
        scratch_shapes=[pltpu.VMEM(PENCILS.shape, jnp.float32), pltpu.SemaphoreType.DMA((2 * NC,))],
    )(accum_z, term_z)


def exchange(a, axis):
    return lax.all_to_all(a, axis, split_axis=0, concat_axis=0, tiled=True)


def col_exchange(a, y, h, term):
    a = a.reshape(4, 4, NC, YB, LN)
    along_z = lambda x, s: lax.ppermute(x, "col", [(i * 4 + j, i * 4 + (j + s) % 4) for i in range(4) for j in range(4)])
    along_y = lambda x, s: lax.ppermute(x, "col", [(i * 4 + j, (i + s) % 4 * 4 + j) for i in range(4) for j in range(4)])
    take = lambda x, i, axis: lax.dynamic_index_in_dim(x, i & 3, axis, keepdims=False)
    odd = [along_z(take(a, h + s, 1), s) for s in (1, 3)]
    even = jnp.stack([take(a, h, 1), take(a, h + 2, 1)], axis=1)
    even = [take(even, y, 0)] + [along_y(take(even, y + t, 0), t) for t in (1, 2, 3)]
    two = along_z(jnp.stack([e[1] for e in even]), 2)
    odd, term = lax.optimization_barrier((odd, term))
    odd = jnp.stack(odd, axis=1)
    odd = [take(odd, y, 0)] + [along_y(take(odd, y + t, 0), t) for t in (1, 2, 3)]
    place = lambda t, s: jnp.where(s & 1, 2 * t + (s >> 1), 8 + 2 * s + t)
    at = [place((y - i) & 3, (h - j) & 3) for i in range(4) for j in range(4)]
    return term, odd, [e[0] for e in even], two, jnp.stack(at).astype(jnp.int32)


def per_device(velocity, dx_matrix, dy_matrix, dz_matrix, metric):
    me = lax.axis_index("col")
    block = me.reshape(1).astype(jnp.int32)
    v = jnp.transpose(velocity, (0, 1, 3, 2))
    v_y = exchange(pack(v), "row")
    part, v_y = lax.optimization_barrier((x_term(block, v, dx_matrix), v_y))
    term = y_term(block, v_y, dy_matrix, metric)
    term, odd, zero, two, at = col_exchange(v_y, me >> 2, me & 3, term)
    accum = exchange(part, "row") + term
    accum, odd, zero, two = lax.optimization_barrier((accum, odd, zero, two))
    accum_z = exchange(accum, "col")
    v_z = jnp.concatenate(odd + [jnp.stack(zero), two])
    return jnp.transpose(finish(accum_z, z_term(at, v_z, dz_matrix)), (0, 3, 1, 2))


def solution(mesh):
    return jax.shard_map(
        per_device,
        mesh=mesh,
        in_specs=(P(None, "col", None, "row"), P(), P(), P(), P()),
        out_specs=P(None, None, "row", "col"),
        check_vma=False,
    )
```

```python
import jax
import jax.numpy as jnp
from jax import lax
from jax.experimental import pallas as pl
from jax.experimental.pallas import tpu as pltpu
from jax.sharding import PartitionSpec as P

NB, NC, YB, LN = 16, 3, 96, 128
ZB, NX, NY = 8, 256, 1536
SIZE = NB * NC * YB * LN * 4
BLOCKS = jax.ShapeDtypeStruct((NB, NC, YB, LN), jnp.float32)
PENCILS = jax.ShapeDtypeStruct((NC, NB, YB, LN), jnp.float32)
VMEM = pl.BlockSpec(memory_space=pltpu.VMEM)
SMEM = pl.BlockSpec(memory_space=pltpu.SMEM)
HBM = pl.BlockSpec(memory_space=pltpu.HBM)


def call(kernel, flops=0, nbytes=0, limit=24, **kw):
    return pl.pallas_call(
        kernel,
        compiler_params=pltpu.CompilerParams(vmem_limit_bytes=limit * 1024 * 1024),
        cost_estimate=pl.CostEstimate(flops=flops, bytes_accessed=nbytes, transcendentals=0),
        **kw,
    )


def lanes8():
    return lax.broadcasted_iota(jnp.int32, (8, LN), 1)


def zx_to_xz(lane, block):
    lane = (lane - 8 * block) & (LN - 1)
    return ((lane & 7) << 4) | (lane & 8) | (lane >> 4)


def over_rows(components, body):
    tiles = YB // 8

    def step(i, _):
        body(components[0] + i // tiles, pl.ds(pl.multiple_of(i % tiles * 8, 8), 8))
        return 0

    lax.fori_loop(0, len(components) * tiles, step, 0, unroll=3)


ALL = range(NC)


def split(v):
    high = v.astype(jnp.bfloat16)
    return high, (v - high.astype(jnp.float32)).astype(jnp.bfloat16)


def dot3(a, b, dims):
    dot = lambda x, y: lax.dot_general(x, y, (dims, ((), ())), preferred_element_type=jnp.float32)
    return dot(a[0], b[0]) + (dot(a[0], b[1]) + dot(a[1], b[0]))


def turn(arrs, width, lane):
    n = len(arrs)
    step = 1
    while step < n:
        high = (lane & width * step) != 0
        arrs = [jnp.where(high, arrs[(i + step) % n], arrs[i]) for i in range(n)]
        step *= 2
    return [pltpu.roll(arrs[-g % n], LN - width * g, 1) if g else arrs[0] for g in range(n)]


def x_to_blocks(load, lane, half):
    arrs = [load(z, half) for z in range(ZB)]
    return turn([pltpu.roll(a, 16 * z, 1) if z else a for z, a in enumerate(arrs)], 16, lane)


def pack_kernel(v_hbm, out_hbm, v_ref, out_ref, sems):
    lane = lanes8()
    loads = [pltpu.make_async_copy(v_hbm.at[c], v_ref.at[c], sems.at[c]) for c in ALL]
    stores = [pltpu.make_async_copy(out_ref.at[c], out_hbm.at[:, c], sems.at[NC + c]) for c in ALL]
    for load in loads:
        load.start()

    def body(c, rows):
        for half in range(2):
            arrs = x_to_blocks(lambda z, h: v_ref[c, z, rows, h * LN : (h + 1) * LN], lane, half)
            for i in range(8):
                out_ref[c, half * 8 + i, rows, :] = arrs[i]

    for c in ALL:
        loads[c].wait()
        over_rows([c], body)
        stores[c].start()
    for store in stores:
        store.wait()


def pack(v):
    return call(
        pack_kernel,
        0,
        2 * SIZE,
        limit=56,
        in_specs=[HBM],
        out_specs=HBM,
        out_shape=BLOCKS,
        scratch_shapes=[
            pltpu.VMEM((NC, ZB, YB, NX), jnp.float32),
            pltpu.VMEM((NC, NB, YB, LN), jnp.float32),
            pltpu.SemaphoreType.DMA((2 * NC,)),
        ],
    )(v)


def x_kernel(block_ref, v_ref, dx_ref, out_ref, part_ref):
    d = split(dx_ref[...])
    for c in range(NC):
        deriv = dot3(split(v_ref[c].reshape(ZB * YB, NX)), d, ((1,), (1,)))
        part_ref[c] = v_ref[0] * deriv.reshape(ZB, YB, NX)
    lane = lanes8()
    order = zx_to_xz(lane, block_ref[0])

    def body(c, rows):
        for half in range(2):
            arrs = x_to_blocks(lambda z, h: part_ref[c, z, rows, h * LN : (h + 1) * LN], lane, half)
            for i in range(8):
                out_ref[half * 8 + i, c, rows, :] = jnp.take_along_axis(arrs[i], order, axis=1)

    over_rows(ALL, body)


def x_term(block, v, dx_matrix):
    return call(
        x_kernel,
        6 * NC * ZB * YB * NX * NX,
        2 * SIZE,
        in_specs=[SMEM, VMEM, VMEM],
        out_specs=VMEM,
        out_shape=BLOCKS,
        scratch_shapes=[pltpu.VMEM((NC, ZB, YB, NX), jnp.float32)],
    )(block, v, dx_matrix)


def y_kernel(block_ref, v_ref, dy_ref, metric_ref, out_ref, vh_ref, vl_ref, t_ref):
    step = pl.program_id(0)

    @pl.when(step == 0)
    def _():
        for c in range(NC):
            high, low = split(v_ref[:, c].reshape(NY, LN))
            vh_ref[:, c * LN : (c + 1) * LN] = high
            vl_ref[:, c * LN : (c + 1) * LN] = low

    nb = out_ref.shape[0]
    deriv = dot3(split(dy_ref[...]), (vh_ref[...], vl_ref[...]), ((1,), (0,)))
    v1 = v_ref[pl.ds(step * nb, nb), 1].reshape(nb * YB, LN) * metric_ref[...]
    for c in range(NC):
        t_ref[:, c] = (v1 * deriv[:, c * LN : (c + 1) * LN]).reshape(nb, YB, LN)
    order = zx_to_xz(lanes8(), block_ref[0])

    def body(c, rows):
        for b in range(nb):
            out_ref[b, c, rows, :] = jnp.take_along_axis(t_ref[b, c, rows, :], order, axis=1)

    over_rows(ALL, body)


def y_term(block, v_y, dy_matrix, metric):
    nb = 4
    return call(
        y_kernel,
        6 * NY * NY * NC * LN,
        2 * SIZE + NY * NY * 4,
        grid=(NB // nb,),
        in_specs=[
            SMEM,
            pl.BlockSpec((NB, NC, YB, LN), lambda i: (0, 0, 0, 0)),
            pl.BlockSpec((nb * YB, NY), lambda i: (i, 0)),
            pl.BlockSpec((nb * YB, LN), lambda i: (i, 0)),
        ],
        out_specs=pl.BlockSpec((nb, NC, YB, LN), lambda i: (i, 0, 0, 0)),
        out_shape=BLOCKS,
        scratch_shapes=[pltpu.VMEM((NY, NC * LN), jnp.bfloat16)] * 2
        + [pltpu.VMEM((nb, NC, YB, LN), jnp.float32)],
    )(block, v_y, dy_matrix, jnp.broadcast_to(metric[:, None], (NY, LN)))


def z_to_lanes(arrs, lane):
    turned = turn(arrs, 8, lane)
    return [turned[(x & 7) * 2 + (x >> 3)] for x in range(NB)]


def z_kernel(at_ref, v_ref, dz_ref, out_ref, t_ref):
    d = split(dz_ref[...])
    lane = lanes8()
    at = [at_ref[s] for s in range(NB)]

    def body(c, rows):
        arrs = [jnp.take_along_axis(v_ref[at[s], c, rows, :], zx_to_xz(lane, s), axis=1) for s in range(NB)]
        arrs = z_to_lanes(arrs, lane)
        for x in range(NB):
            t_ref[c, x, rows, :] = arrs[x]

    over_rows(ALL, body)
    for c in range(NC):
        deriv = dot3(split(t_ref[c].reshape(NB * YB, LN)), d, ((1,), (1,)))
        out_ref[c] = t_ref[2] * deriv.reshape(NB, YB, LN)


def z_term(at, v_z, dz_matrix):
    return call(
        z_kernel,
        6 * NC * NB * YB * LN * LN,
        2 * SIZE,
        in_specs=[SMEM, VMEM, VMEM],
        out_specs=VMEM,
        out_shape=PENCILS,
        scratch_shapes=[pltpu.VMEM((NC, NB, YB, LN), jnp.float32)],
    )(at, v_z, dz_matrix)


def finish_kernel(a_ref, w_hbm, out_hbm, w_ref, sems):
    lane = lanes8()
    loads = [pltpu.make_async_copy(w_hbm.at[c], w_ref.at[c], sems.at[c]) for c in ALL]
    stores = [pltpu.make_async_copy(w_ref.at[c], out_hbm.at[c], sems.at[NC + c]) for c in ALL]
    for load in loads:
        load.start()

    def body(c, rows):
        arrs = z_to_lanes([a_ref[s, c, rows, :] for s in range(NB)], lane)
        for x in range(NB):
            w_ref[c, x, rows, :] += arrs[x]

    for c in ALL:
        loads[c].wait()
        over_rows([c], body)
        stores[c].start()
    for store in stores:
        store.wait()


def finish(accum_z, term_z):
    return call(
        finish_kernel,
        0,
        3 * SIZE,
        in_specs=[VMEM, HBM],
        out_specs=HBM,
        out_shape=PENCILS,
        scratch_shapes=[pltpu.VMEM(PENCILS.shape, jnp.float32), pltpu.SemaphoreType.DMA((2 * NC,))],
    )(accum_z, term_z)


def exchange(a, axis):
    return lax.all_to_all(a, axis, split_axis=0, concat_axis=0, tiled=True)


def col_exchange(a, y, h, term):
    a = a.reshape(4, 4, NC, YB, LN)
    along_z = lambda x, s: lax.ppermute(x, "col", [(i * 4 + j, i * 4 + (j + s) % 4) for i in range(4) for j in range(4)])
    along_y = lambda x, s: lax.ppermute(x, "col", [(i * 4 + j, (i + s) % 4 * 4 + j) for i in range(4) for j in range(4)])
    take = lambda x, i, axis: lax.dynamic_index_in_dim(x, i & 3, axis, keepdims=False)
    odd = [along_z(take(a, h + s, 1), s) for s in (1, 3)]
    even = jnp.stack([take(a, h, 1), take(a, h + 2, 1)], axis=1)
    even = [take(even, y, 0)] + [along_y(take(even, y + t, 0), t) for t in (1, 2, 3)]
    two = along_z(jnp.stack([e[1] for e in even]), 2)
    odd, term = lax.optimization_barrier((odd, term))
    odd = jnp.stack(odd, axis=1)
    odd = [take(odd, y, 0)] + [along_y(take(odd, y + t, 0), t) for t in (1, 2, 3)]
    place = lambda t, s: jnp.where(s & 1, 2 * t + (s >> 1), 8 + 2 * s + t)
    at = [place((y - i) & 3, (h - j) & 3) for i in range(4) for j in range(4)]
    return term, odd, [e[0] for e in even], two, jnp.stack(at).astype(jnp.int32)


def per_device(velocity, dx_matrix, dy_matrix, dz_matrix, metric):
    me = lax.axis_index("col")
    block = me.reshape(1).astype(jnp.int32)
    v = jnp.transpose(velocity, (0, 1, 3, 2))
    v_y = exchange(pack(v), "row")
    part, v_y = lax.optimization_barrier((x_term(block, v, dx_matrix), v_y))
    term = y_term(block, v_y, dy_matrix, metric)
    term, odd, zero, two, at = col_exchange(v_y, me >> 2, me & 3, term)
    accum = exchange(part, "row") + term
    accum, odd, zero, two = lax.optimization_barrier((accum, odd, zero, two))
    accum_z = exchange(accum, "col")
    v_z = jnp.concatenate(odd + [jnp.stack(zero), two])
    return jnp.transpose(finish(accum_z, z_term(at, v_z, dz_matrix)), (0, 3, 1, 2))


def solution(mesh):
    return jax.shard_map(
        per_device,
        mesh=mesh,
        in_specs=(P(None, "col", None, "row"), P(), P(), P(), P()),
        out_specs=P(None, None, "row", "col"),
        check_vma=False,
    )
```

```python
import jax
import jax.numpy as jnp
from jax import lax
from jax.experimental import pallas as pl
from jax.experimental.pallas import tpu as pltpu
from jax.sharding import PartitionSpec as P

NB, NC, YB, LN = 16, 3, 96, 128
ZB, NX, NY = 8, 256, 1536
SIZE = NB * NC * YB * LN * 4
BLOCKS = jax.ShapeDtypeStruct((NB, NC, YB, LN), jnp.float32)
TERMS = jax.ShapeDtypeStruct((28 * NC, NB, YB, LN), jnp.float32)
PENCILS = jax.ShapeDtypeStruct((NC, NB, YB, LN), jnp.float32)
VMEM = pl.BlockSpec(memory_space=pltpu.VMEM)
SMEM = pl.BlockSpec(memory_space=pltpu.SMEM)
HBM = pl.BlockSpec(memory_space=pltpu.HBM)


def call(kernel, flops=0, nbytes=0, limit=24, **kw):
    return pl.pallas_call(
        kernel,
        compiler_params=pltpu.CompilerParams(vmem_limit_bytes=limit * 1024 * 1024),
        cost_estimate=pl.CostEstimate(flops=flops, bytes_accessed=nbytes, transcendentals=0),
        **kw,
    )


def lanes8():
    return lax.broadcasted_iota(jnp.int32, (8, LN), 1)


def zx_to_xz(lane, block):
    lane = (lane - 8 * block) & (LN - 1)
    return ((lane & 7) << 4) | (lane & 8) | (lane >> 4)


def over_rows(components, body):
    tiles = YB // 8

    def step(i, _):
        body(components[0] + i // tiles, pl.ds(pl.multiple_of(i % tiles * 8, 8), 8))
        return 0

    lax.fori_loop(0, len(components) * tiles, step, 0, unroll=3)


ALL = range(NC)


def split(v):
    high = v.astype(jnp.bfloat16)
    return high, (v - high.astype(jnp.float32)).astype(jnp.bfloat16)


def dot3(a, b, dims):
    dot = lambda x, y: lax.dot_general(x, y, (dims, ((), ())), preferred_element_type=jnp.float32)
    return dot(a[0], b[0]) + (dot(a[0], b[1]) + dot(a[1], b[0]))


def turn(arrs, width, lane):
    n = len(arrs)
    step = 1
    while step < n:
        high = (lane & width * step) != 0
        arrs = [jnp.where(high, arrs[(i + step) % n], arrs[i]) for i in range(n)]
        step *= 2
    return [pltpu.roll(arrs[-g % n], LN - width * g, 1) if g else arrs[0] for g in range(n)]


def x_to_blocks(load, lane, half):
    arrs = [load(z, half) for z in range(ZB)]
    return turn([pltpu.roll(a, 16 * z, 1) if z else a for z, a in enumerate(arrs)], 16, lane)


def pack_kernel(v_hbm, out_hbm, v_ref, out_ref, sems):
    lane = lanes8()
    loads = [pltpu.make_async_copy(v_hbm.at[c], v_ref.at[c], sems.at[c]) for c in ALL]
    stores = [pltpu.make_async_copy(out_ref.at[c], out_hbm.at[:, c], sems.at[NC + c]) for c in ALL]
    for load in loads:
        load.start()

    def body(c, rows):
        for half in range(2):
            arrs = x_to_blocks(lambda z, h: v_ref[c, z, rows, h * LN : (h + 1) * LN], lane, half)
            for i in range(8):
                out_ref[c, half * 8 + i, rows, :] = arrs[i]

    for c in ALL:
        loads[c].wait()
        over_rows([c], body)
        stores[c].start()
    for store in stores:
        store.wait()


def pack(v):
    return call(
        pack_kernel,
        0,
        2 * SIZE,
        limit=56,
        in_specs=[HBM],
        out_specs=HBM,
        out_shape=BLOCKS,
        scratch_shapes=[
            pltpu.VMEM((NC, ZB, YB, NX), jnp.float32),
            pltpu.VMEM((NC, NB, YB, LN), jnp.float32),
            pltpu.SemaphoreType.DMA((2 * NC,)),
        ],
    )(v)


def x_kernel(block_ref, v_ref, dx_ref, out_ref, part_ref):
    d = split(dx_ref[...])
    for c in range(NC):
        deriv = dot3(split(v_ref[c].reshape(ZB * YB, NX)), d, ((1,), (1,)))
        part_ref[c] = v_ref[0] * deriv.reshape(ZB, YB, NX)
    lane = lanes8()
    order = zx_to_xz(lane, block_ref[0])

    def body(c, rows):
        for half in range(2):
            arrs = x_to_blocks(lambda z, h: part_ref[c, z, rows, h * LN : (h + 1) * LN], lane, half)
            for i in range(8):
                out_ref[half * 8 + i, c, rows, :] = jnp.take_along_axis(arrs[i], order, axis=1)

    over_rows(ALL, body)


def x_term(block, v, dx_matrix):
    return call(
        x_kernel,
        6 * NC * ZB * YB * NX * NX,
        2 * SIZE,
        in_specs=[SMEM, VMEM, VMEM],
        out_specs=VMEM,
        out_shape=BLOCKS,
        scratch_shapes=[pltpu.VMEM((NC, ZB, YB, NX), jnp.float32)],
    )(block, v, dx_matrix)


def y_kernel(block_ref, v_ref, dy_ref, metric_ref, out_ref, vh_ref, vl_ref, t_ref):
    step = pl.program_id(0)

    @pl.when(step == 0)
    def _():
        for c in range(NC):
            high, low = split(v_ref[:, c].reshape(NY, LN))
            vh_ref[:, c * LN : (c + 1) * LN] = high
            vl_ref[:, c * LN : (c + 1) * LN] = low

    nb = out_ref.shape[0]
    deriv = dot3(split(dy_ref[...]), (vh_ref[...], vl_ref[...]), ((1,), (0,)))
    v1 = v_ref[pl.ds(step * nb, nb), 1].reshape(nb * YB, LN) * metric_ref[...]
    for c in range(NC):
        t_ref[:, c] = (v1 * deriv[:, c * LN : (c + 1) * LN]).reshape(nb, YB, LN)
    order = zx_to_xz(lanes8(), block_ref[0])

    def body(c, rows):
        for b in range(nb):
            out_ref[b, c, rows, :] = jnp.take_along_axis(t_ref[b, c, rows, :], order, axis=1)

    over_rows(ALL, body)


def y_term(block, v_y, dy_matrix, metric):
    nb = 4
    return call(
        y_kernel,
        6 * NY * NY * NC * LN,
        2 * SIZE + NY * NY * 4,
        grid=(NB // nb,),
        in_specs=[
            SMEM,
            pl.BlockSpec((NB, NC, YB, LN), lambda i: (0, 0, 0, 0)),
            pl.BlockSpec((nb * YB, NY), lambda i: (i, 0)),
            pl.BlockSpec((nb * YB, LN), lambda i: (i, 0)),
        ],
        out_specs=pl.BlockSpec((nb, NC, YB, LN), lambda i: (i, 0, 0, 0)),
        out_shape=BLOCKS,
        scratch_shapes=[pltpu.VMEM((NY, NC * LN), jnp.bfloat16)] * 2
        + [pltpu.VMEM((nb, NC, YB, LN), jnp.float32)],
    )(block, v_y, dy_matrix, jnp.broadcast_to(metric[:, None], (NY, LN)))


def z_to_lanes(arrs, lane):
    turned = turn(arrs, 8, lane)
    return [turned[(x & 7) * 2 + (x >> 3)] for x in range(NB)]


def z_kernel(at_ref, v_ref, dz_ref, out_hbm, t_ref, out_ref, sems):
    d = split(dz_ref[...])
    lane = lanes8()
    at = [at_ref[s] for s in range(NB)]

    def body(c, rows):
        arrs = [jnp.take_along_axis(v_ref[at[s], c, rows, :], zx_to_xz(lane, s), axis=1) for s in range(NB)]
        arrs = z_to_lanes(arrs, lane)
        for x in range(NB):
            t_ref[c, x, rows, :] = arrs[x]

    over_rows(ALL, body)
    stores = []
    for c in ALL:
        deriv = dot3(split(t_ref[c].reshape(NB * YB, LN)), d, ((1,), (1,)))
        out_ref[c] = t_ref[2] * deriv.reshape(NB, YB, LN)
        stores.append(pltpu.make_async_copy(out_ref.at[c], out_hbm.at[c], sems.at[c]))
        stores[c].start()
    for store in stores:
        store.wait()


def z_term(at, v_z, dz_matrix):
    return call(
        z_kernel,
        6 * NC * NB * YB * LN * LN,
        2 * SIZE,
        in_specs=[SMEM, VMEM, VMEM],
        out_specs=HBM,
        out_shape=TERMS,
        scratch_shapes=[pltpu.VMEM(PENCILS.shape, jnp.float32)] * 2 + [pltpu.SemaphoreType.DMA((NC,))],
    )(at, v_z, dz_matrix)


def finish_kernel(a_ref, w_hbm, out_hbm, w_ref, sems):
    lane = lanes8()
    loads = [pltpu.make_async_copy(w_hbm.at[c], w_ref.at[c], sems.at[c]) for c in ALL]
    stores = [pltpu.make_async_copy(w_ref.at[c], out_hbm.at[c], sems.at[NC + c]) for c in ALL]
    for load in loads:
        load.start()

    def body(c, rows):
        arrs = z_to_lanes([a_ref[s, c, rows, :] for s in range(NB)], lane)
        for x in range(NB):
            w_ref[c, x, rows, :] += arrs[x]

    for c in ALL:
        loads[c].wait()
        over_rows([c], body)
        stores[c].start()
    for store in stores:
        store.wait()


def finish(accum_z, term_z):
    return call(
        finish_kernel,
        0,
        3 * SIZE,
        in_specs=[VMEM, HBM],
        out_specs=HBM,
        out_shape=PENCILS,
        scratch_shapes=[pltpu.VMEM(PENCILS.shape, jnp.float32), pltpu.SemaphoreType.DMA((2 * NC,))],
    )(accum_z, term_z)


def exchange(a, axis):
    return lax.all_to_all(a, axis, split_axis=0, concat_axis=0, tiled=True)


def col_exchange(a, y, h, term):
    a = a.reshape(4, 4, NC, YB, LN)
    along_z = lambda x, s: lax.ppermute(x, "col", [(i * 4 + j, i * 4 + (j + s) % 4) for i in range(4) for j in range(4)])
    along_y = lambda x, s: lax.ppermute(x, "col", [(i * 4 + j, (i + s) % 4 * 4 + j) for i in range(4) for j in range(4)])
    take = lambda x, i, axis: lax.dynamic_index_in_dim(x, i & 3, axis, keepdims=False)
    odd = [along_z(take(a, h + s, 1), s) for s in (1, 3)]
    even = jnp.stack([take(a, h, 1), take(a, h + 2, 1)], axis=1)
    even = [take(even, y, 0)] + [along_y(take(even, y + t, 0), t) for t in (1, 2, 3)]
    two = along_z(jnp.stack([e[1] for e in even]), 2)
    odd, term = lax.optimization_barrier((odd, term))
    odd = jnp.stack(odd, axis=1)
    odd = [take(odd, y, 0)] + [along_y(take(odd, y + t, 0), t) for t in (1, 2, 3)]
    place = lambda t, s: jnp.where(s & 1, 2 * t + (s >> 1), 8 + 2 * s + t)
    at = [place((y - i) & 3, (h - j) & 3) for i in range(4) for j in range(4)]
    return term, odd, [e[0] for e in even], two, jnp.stack(at).astype(jnp.int32)


def per_device(velocity, dx_matrix, dy_matrix, dz_matrix, metric):
    me = lax.axis_index("col")
    block = me.reshape(1).astype(jnp.int32)
    v = jnp.transpose(velocity, (0, 1, 3, 2))
    v_y = exchange(pack(v), "row")
    part, v_y = lax.optimization_barrier((x_term(block, v, dx_matrix), v_y))
    term = y_term(block, v_y, dy_matrix, metric)
    term, odd, zero, two, at = col_exchange(v_y, me >> 2, me & 3, term)
    accum = exchange(part, "row") + term
    accum, odd, zero, two = lax.optimization_barrier((accum, odd, zero, two))
    accum_z = exchange(accum, "col")
    v_z = jnp.concatenate(odd + [jnp.stack(zero), two])
    return jnp.transpose(finish(accum_z, z_term(at, v_z, dz_matrix)), (0, 3, 1, 2))


def solution(mesh):
    return jax.shard_map(
        per_device,
        mesh=mesh,
        in_specs=(P(None, "col", None, "row"), P(), P(), P(), P()),
        out_specs=P(None, None, "row", "col"),
        check_vma=False,
    )
```

```python
import jax
import jax.numpy as jnp
from jax import lax
from jax.experimental import pallas as pl
from jax.experimental.pallas import tpu as pltpu
from jax.sharding import PartitionSpec as P

NB, NC, YB, LN = 16, 3, 96, 128
ZB, NX, NY = 8, 256, 1536
SIZE = NB * NC * YB * LN * 4
BLOCKS = jax.ShapeDtypeStruct((NB, NC, YB, LN), jnp.float32)
TERMS = jax.ShapeDtypeStruct((28 * NC, NB, YB, LN), jnp.float32)
PENCILS = jax.ShapeDtypeStruct((NC, NB, YB, LN), jnp.float32)
VMEM = pl.BlockSpec(memory_space=pltpu.VMEM)
SMEM = pl.BlockSpec(memory_space=pltpu.SMEM)
HBM = pl.BlockSpec(memory_space=pltpu.HBM)


def call(kernel, flops=0, nbytes=0, limit=24, **kw):
    return pl.pallas_call(
        kernel,
        compiler_params=pltpu.CompilerParams(vmem_limit_bytes=limit * 1024 * 1024),
        cost_estimate=pl.CostEstimate(flops=flops, bytes_accessed=nbytes, transcendentals=0),
        **kw,
    )


def lanes8():
    return lax.broadcasted_iota(jnp.int32, (8, LN), 1)


def zx_to_xz(lane, block):
    lane = (lane - 8 * block) & (LN - 1)
    return ((lane & 7) << 4) | (lane & 8) | (lane >> 4)


def over_rows(components, body, first=0, count=YB):
    tiles = count // 8

    def step(i, _):
        body(components[0] + i // tiles, pl.ds(pl.multiple_of(first + i % tiles * 8, 8), 8))
        return 0

    lax.fori_loop(0, len(components) * tiles, step, 0, unroll=3)


ALL = range(NC)
HALF = YB // 2
HALVES = [(c, first) for c in ALL for first in (0, HALF)]


def split(v):
    high = v.astype(jnp.bfloat16)
    return high, (v - high.astype(jnp.float32)).astype(jnp.bfloat16)


def dot3(a, b, dims):
    dot = lambda x, y: lax.dot_general(x, y, (dims, ((), ())), preferred_element_type=jnp.float32)
    return dot(a[0], b[0]) + (dot(a[0], b[1]) + dot(a[1], b[0]))


def turn(arrs, width, lane):
    n = len(arrs)
    step = 1
    while step < n:
        high = (lane & width * step) != 0
        arrs = [jnp.where(high, arrs[(i + step) % n], arrs[i]) for i in range(n)]
        step *= 2
    return [pltpu.roll(arrs[-g % n], LN - width * g, 1) if g else arrs[0] for g in range(n)]


def x_to_blocks(load, lane, half):
    arrs = [load(z, half) for z in range(ZB)]
    return turn([pltpu.roll(a, 16 * z, 1) if z else a for z, a in enumerate(arrs)], 16, lane)


def pack_kernel(v_hbm, out_hbm, v_ref, out_ref, sems):
    lane = lanes8()
    loads, stores = [], []
    for i, (c, first) in enumerate(HALVES):
        rows = pl.ds(first, HALF)
        loads.append(pltpu.make_async_copy(v_hbm.at[c, :, rows], v_ref.at[c, :, rows], sems.at[i]))
        stores.append(pltpu.make_async_copy(out_ref.at[c, :, rows], out_hbm.at[:, c, rows], sems.at[len(HALVES) + i]))
    for load in loads:
        load.start()

    def body(c, rows):
        for half in range(2):
            arrs = x_to_blocks(lambda z, h: v_ref[c, z, rows, h * LN : (h + 1) * LN], lane, half)
            for i in range(8):
                out_ref[c, half * 8 + i, rows, :] = arrs[i]

    for i, (c, first) in enumerate(HALVES):
        loads[i].wait()
        over_rows([c], body, first, HALF)
        stores[i].start()
    for store in stores:
        store.wait()


def pack(v):
    return call(
        pack_kernel,
        0,
        2 * SIZE,
        limit=56,
        in_specs=[HBM],
        out_specs=HBM,
        out_shape=BLOCKS,
        scratch_shapes=[
            pltpu.VMEM((NC, ZB, YB, NX), jnp.float32),
            pltpu.VMEM((NC, NB, YB, LN), jnp.float32),
            pltpu.SemaphoreType.DMA((2 * len(HALVES),)),
        ],
    )(v)


def x_kernel(block_ref, v_ref, dx_ref, out_ref, part_ref):
    d = split(dx_ref[...])
    for c in range(NC):
        deriv = dot3(split(v_ref[c].reshape(ZB * YB, NX)), d, ((1,), (1,)))
        part_ref[c] = v_ref[0] * deriv.reshape(ZB, YB, NX)
    lane = lanes8()
    order = zx_to_xz(lane, block_ref[0])

    def body(c, rows):
        for half in range(2):
            arrs = x_to_blocks(lambda z, h: part_ref[c, z, rows, h * LN : (h + 1) * LN], lane, half)
            for i in range(8):
                out_ref[half * 8 + i, c, rows, :] = jnp.take_along_axis(arrs[i], order, axis=1)

    over_rows(ALL, body)


def x_term(block, v, dx_matrix):
    return call(
        x_kernel,
        6 * NC * ZB * YB * NX * NX,
        2 * SIZE,
        in_specs=[SMEM, VMEM, VMEM],
        out_specs=VMEM,
        out_shape=BLOCKS,
        scratch_shapes=[pltpu.VMEM((NC, ZB, YB, NX), jnp.float32)],
    )(block, v, dx_matrix)


def y_kernel(block_ref, v_ref, dy_ref, metric_ref, out_ref, vh_ref, vl_ref, t_ref):
    step = pl.program_id(0)

    @pl.when(step == 0)
    def _():
        for c in range(NC):
            high, low = split(v_ref[:, c].reshape(NY, LN))
            vh_ref[:, c * LN : (c + 1) * LN] = high
            vl_ref[:, c * LN : (c + 1) * LN] = low

    nb = out_ref.shape[0]
    deriv = dot3(split(dy_ref[...]), (vh_ref[...], vl_ref[...]), ((1,), (0,)))
    v1 = v_ref[pl.ds(step * nb, nb), 1].reshape(nb * YB, LN) * metric_ref[...]
    for c in range(NC):
        t_ref[:, c] = (v1 * deriv[:, c * LN : (c + 1) * LN]).reshape(nb, YB, LN)
    order = zx_to_xz(lanes8(), block_ref[0])

    def body(c, rows):
        for b in range(nb):
            out_ref[b, c, rows, :] = jnp.take_along_axis(t_ref[b, c, rows, :], order, axis=1)

    over_rows(ALL, body)


def y_term(block, v_y, dy_matrix, metric):
    nb = 4
    return call(
        y_kernel,
        6 * NY * NY * NC * LN,
        2 * SIZE + NY * NY * 4,
        grid=(NB // nb,),
        in_specs=[
            SMEM,
            pl.BlockSpec((NB, NC, YB, LN), lambda i: (0, 0, 0, 0)),
            pl.BlockSpec((nb * YB, NY), lambda i: (i, 0)),
            pl.BlockSpec((nb * YB, LN), lambda i: (i, 0)),
        ],
        out_specs=pl.BlockSpec((nb, NC, YB, LN), lambda i: (i, 0, 0, 0)),
        out_shape=BLOCKS,
        scratch_shapes=[pltpu.VMEM((NY, NC * LN), jnp.bfloat16)] * 2
        + [pltpu.VMEM((nb, NC, YB, LN), jnp.float32)],
    )(block, v_y, dy_matrix, jnp.broadcast_to(metric[:, None], (NY, LN)))


def z_to_lanes(arrs, lane):
    turned = turn(arrs, 8, lane)
    return [turned[(x & 7) * 2 + (x >> 3)] for x in range(NB)]


def z_kernel(at_ref, v_ref, dz_ref, out_hbm, t_ref, out_ref, sems):
    d = split(dz_ref[...])
    lane = lanes8()
    at = [at_ref[s] for s in range(NB)]

    def body(c, rows):
        arrs = [jnp.take_along_axis(v_ref[at[s], c, rows, :], zx_to_xz(lane, s), axis=1) for s in range(NB)]
        arrs = z_to_lanes(arrs, lane)
        for x in range(NB):
            t_ref[c, x, rows, :] = arrs[x]

    over_rows(ALL, body)
    stores = []
    for c in ALL:
        deriv = dot3(split(t_ref[c].reshape(NB * YB, LN)), d, ((1,), (1,)))
        out_ref[c] = t_ref[2] * deriv.reshape(NB, YB, LN)
        stores.append(pltpu.make_async_copy(out_ref.at[c], out_hbm.at[c], sems.at[c]))
        stores[c].start()
    for store in stores:
        store.wait()


def z_term(at, v_z, dz_matrix):
    return call(
        z_kernel,
        6 * NC * NB * YB * LN * LN,
        2 * SIZE,
        in_specs=[SMEM, VMEM, VMEM],
        out_specs=HBM,
        out_shape=TERMS,
        scratch_shapes=[pltpu.VMEM(PENCILS.shape, jnp.float32)] * 2 + [pltpu.SemaphoreType.DMA((NC,))],
    )(at, v_z, dz_matrix)


def finish_kernel(a_ref, w_hbm, out_hbm, w_ref, sems):
    lane = lanes8()
    loads, stores = [], []
    for i, (c, first) in enumerate(HALVES):
        rows = pl.ds(first, HALF)
        loads.append(pltpu.make_async_copy(w_hbm.at[c, :, rows], w_ref.at[c, :, rows], sems.at[i]))
        stores.append(pltpu.make_async_copy(w_ref.at[c, :, rows], out_hbm.at[c, :, rows], sems.at[len(HALVES) + i]))
    for load in loads:
        load.start()

    def body(c, rows):
        arrs = z_to_lanes([a_ref[s, c, rows, :] for s in range(NB)], lane)
        for x in range(NB):
            w_ref[c, x, rows, :] += arrs[x]

    for i, (c, first) in enumerate(HALVES):
        loads[i].wait()
        over_rows([c], body, first, HALF)
        stores[i].start()
    for store in stores:
        store.wait()


def finish(accum_z, term_z):
    return call(
        finish_kernel,
        0,
        3 * SIZE,
        in_specs=[VMEM, HBM],
        out_specs=HBM,
        out_shape=PENCILS,
        scratch_shapes=[pltpu.VMEM(PENCILS.shape, jnp.float32), pltpu.SemaphoreType.DMA((2 * len(HALVES),))],
    )(accum_z, term_z)


def exchange(a, axis):
    return lax.all_to_all(a, axis, split_axis=0, concat_axis=0, tiled=True)


def col_exchange(a, y, h, term):
    a = a.reshape(4, 4, NC, YB, LN)
    along_z = lambda x, s: lax.ppermute(x, "col", [(i * 4 + j, i * 4 + (j + s) % 4) for i in range(4) for j in range(4)])
    along_y = lambda x, s: lax.ppermute(x, "col", [(i * 4 + j, (i + s) % 4 * 4 + j) for i in range(4) for j in range(4)])
    take = lambda x, i, axis: lax.dynamic_index_in_dim(x, i & 3, axis, keepdims=False)
    odd = [along_z(take(a, h + s, 1), s) for s in (1, 3)]
    even = jnp.stack([take(a, h, 1), take(a, h + 2, 1)], axis=1)
    even = [take(even, y, 0)] + [along_y(take(even, y + t, 0), t) for t in (1, 2, 3)]
    two = along_z(jnp.stack([e[1] for e in even]), 2)
    odd, term = lax.optimization_barrier((odd, term))
    odd = jnp.stack(odd, axis=1)
    odd = [take(odd, y, 0)] + [along_y(take(odd, y + t, 0), t) for t in (1, 2, 3)]
    place = lambda t, s: jnp.where(s & 1, 2 * t + (s >> 1), 8 + 2 * s + t)
    at = [place((y - i) & 3, (h - j) & 3) for i in range(4) for j in range(4)]
    return term, odd, [e[0] for e in even], two, jnp.stack(at).astype(jnp.int32)


def per_device(velocity, dx_matrix, dy_matrix, dz_matrix, metric):
    me = lax.axis_index("col")
    block = me.reshape(1).astype(jnp.int32)
    v = jnp.transpose(velocity, (0, 1, 3, 2))
    v_y = exchange(pack(v), "row")
    part, v_y = lax.optimization_barrier((x_term(block, v, dx_matrix), v_y))
    term = y_term(block, v_y, dy_matrix, metric)
    term, odd, zero, two, at = col_exchange(v_y, me >> 2, me & 3, term)
    accum = exchange(part, "row") + term
    accum, odd, zero, two = lax.optimization_barrier((accum, odd, zero, two))
    accum_z = exchange(accum, "col")
    v_z = jnp.concatenate(odd + [jnp.stack(zero), two])
    return jnp.transpose(finish(accum_z, z_term(at, v_z, dz_matrix)), (0, 3, 1, 2))


def solution(mesh):
    return jax.shard_map(
        per_device,
        mesh=mesh,
        in_specs=(P(None, "col", None, "row"), P(), P(), P(), P()),
        out_specs=P(None, None, "row", "col"),
        check_vma=False,
    )
```
